256 devices in a mesh: tm: 16 (over z, core), mesh: 16 (over y, x).
Axes of the slice: x: 4, y: 4, z: 8, core: 2. Of those that a mesh axis runs over, the one named last changes fastest.
Arguments:
- trajectory: bfloat16 [16, 2560, 512], P('tm', 'mesh'), may hold values from -6 to 6
- increments: bfloat16 [16, 2560, 512], P('tm', 'mesh'), may hold values from -6 to 6
- weight_send: bfloat16 [512, 512], replicated, may hold values from -0.25 to 0.25
- weight_receive: bfloat16 [512, 512], replicated, may hold values from -0.25 to 0.25
- weight_message: bfloat16 [512, 512], replicated, may hold values from -0.25 to 0.25
- weight_node: bfloat16 [512, 512], replicated, may hold values from -0.25 to 0.25
- weight_inbox: bfloat16 [512, 512], replicated, may hold values from -0.09375 to 0.09375
- weight_output: bfloat16 [512, 512], replicated, may hold values from -0.25 to 0.25
- senders: int32 [20480], P('mesh'), may hold values from 0 to 415, as said below
- receivers: int32 [20480], P('mesh'), may hold values from 0 to 159
- send_table: int32 [4096], P('mesh'), may hold values from -1 to 159, as said below
Outputs:
- forward_image: bfloat16 [16, 2560, 512], P('tm', 'mesh')
- normal_image: bfloat16 [16, 2560, 512], P('tm', 'mesh')
The draws below stay inside these ranges and needn't reach their ends.
Inputs may be any that keep to these rules, and one draw needn't show every extreme that they name: `send_table`: entries (p * 16 + q) * 16 to (p * 16 + q + 1) * 16 - 1 list distinct local nodes of partition p needed by partition q, followed by -1 padding; a partition lists nothing to itself; every partition fills all 16 slots towards some partition and receives 16 filled slots from some partition. `senders`: values below 160 are the partition's own nodes; a value 160 + p * 16 + s names slot s of the list partition p sends to this partition, and that slot is never padding.
All inputs are finite; a program needn't handle non-finite values.
Results may differ from the reference program's by a relative error of at most 0.013.
Values may be sent and summed in bfloat16 or wider, within the bound.
A program may use at most 64 MiB of HBM per device.

```python
import jax
import jax.numpy as jnp
from jax import lax

D = 512
NODE_DEV = 160
HALO = 16
EDGE_DEV = 1280
REGIONS = 16
SLOTS = 16
NODES = 2560
EDGES = 20480


def halo_counts(key):
    key = jax.random.fold_in(key, 101)
    counts = jax.random.randint(key, (REGIONS, REGIONS), HALO // 4, HALO + 1)
    node_ids = jnp.arange(REGIONS)
    full_pair = node_ids[None, :] == (node_ids[:, None] + 1) % REGIONS
    counts = jnp.where(full_pair, HALO, counts)
    return jnp.where(node_ids[:, None] == node_ids[None, :], 0, counts)


def shuffled(key_row):
    return jax.random.permutation(key_row, NODE_DEV)


def draw_send_table(key, part):
    counts = halo_counts(key)
    key = jax.random.fold_in(key, 3)
    key_list = jax.random.split(key, REGIONS * REGIONS)
    orderings = jax.vmap(shuffled)(key_list)[:, :HALO]
    row_ids = jnp.arange(REGIONS * REGIONS)
    rotation = jnp.where(row_ids == 1, NODE_DEV - 1 - orderings[:, 0], 0)
    orderings = (orderings + rotation[:, None]) % NODE_DEV
    slot_ids = jnp.arange(HALO)
    send_rows = jnp.where(slot_ids[None, :] < counts.reshape(-1)[:, None], orderings, -1)
    return send_rows.reshape(-1).astype(jnp.int32)


def draw_senders(key, part):
    counts = halo_counts(key)
    key = jax.random.fold_in(key, 5)
    key_local, key_pick, key_source, key_slot = jax.random.split(key, 4)
    owner_part = jnp.arange(EDGES) // EDGE_DEV
    position = jnp.arange(EDGES) % EDGE_DEV
    local_ids = jax.random.randint(key_local, (EDGES,), 0, NODE_DEV)
    local_ids = jnp.where(position == 1, 0, local_ids)
    choose_halo = jax.random.randint(key_pick, (EDGES,), 0, 2)
    choose_halo = jnp.where(position == 0, 1, jnp.where(position == 1, 0, choose_halo))
    source = (owner_part + 1 + jax.random.randint(key_source, (EDGES,), 0, REGIONS - 1)) % REGIONS
    source = jnp.where(position == 0, (owner_part + REGIONS - 1) % REGIONS, source)
    limit = jnp.maximum(counts[source, owner_part], 1)
    slot_ids = jax.random.randint(key_slot, (EDGES,), 0, 4 * HALO) % limit
    slot_ids = jnp.where(position == 0, HALO - 1, slot_ids)
    halo_ids = NODE_DEV + source * HALO + slot_ids
    return jnp.where(choose_halo == 1, halo_ids, local_ids).astype(jnp.int32)


def touch_ends(array, stream_key, smallest, high):
    dims = array.shape
    index_at = [jax.random.randint(jax.random.fold_in(stream_key, axis), (), 0, dims[axis]) for axis in range(len(dims))]
    array = array.at[tuple(index_at)].set(smallest)
    longest = dims.index(max(dims))
    index_at[longest] = (index_at[longest] + 1) % dims[longest]
    return array.at[tuple(index_at)].set(high)


def level_of(own_key, dims, cuts, least, largest):
    def one(axis_at, blocks):
        draws = jax.random.uniform(jax.random.fold_in(jax.random.fold_in(own_key, 6), axis_at), (blocks,), jnp.float32, least / len(cuts), largest / len(cuts))
        return jnp.repeat(jnp.exp(draws), dims[axis_at] // blocks).reshape((-1,) + (1,) * (len(dims) - axis_at - 1))

    loudness = one(*cuts[0])
    for cut in cuts[1:]:
        loudness = loudness * one(*cut)
    return loudness


def bell_draw(rng, shape, deviation, most, pieces=(), held_as=jnp.bfloat16):
    values = jax.random.normal(rng, shape, jnp.float32) * deviation
    if len(pieces) > 0:
        values = level_of(rng, shape, pieces, -0.22, 0.18) * values
    return jnp.clip(values, min=-most, max=most).astype(held_as)


def setup_inputs(seed: int = 0) -> dict:
    arg_keys = jax.random.split(jax.random.key(seed), 12)
    return {
        "trajectory": bell_draw(arg_keys[0], (SLOTS, NODES, D), 1.0, 6.0, ((0, 16), (1, 16))),
        "increments": bell_draw(arg_keys[1], (SLOTS, NODES, D), 1.0, 6.0, ((0, 16), (1, 16))),
        "weight_send": bell_draw(arg_keys[2], (D, D), D ** -0.5, 0.25),
        "weight_receive": bell_draw(arg_keys[3], (D, D), D ** -0.5, 0.25),
        "weight_message": bell_draw(arg_keys[4], (D, D), D ** -0.5, 0.25),
        "weight_node": bell_draw(arg_keys[5], (D, D), D ** -0.5, 0.25),
        "weight_inbox": bell_draw(arg_keys[6], (D, D), (8 * D) ** -0.5, 0.09375),
        "weight_output": bell_draw(arg_keys[7], (D, D), D ** -0.5, 0.25),
        "senders": draw_senders(jax.random.fold_in(arg_keys[11], 71), 0),
        "receivers": touch_ends(jax.random.randint(arg_keys[9], (EDGES,), 0, NODE_DEV), jax.random.fold_in(arg_keys[9], 1), 0, NODE_DEV - 1).astype(jnp.int32),
        "send_table": draw_send_table(jax.random.fold_in(arg_keys[11], 71), 0),
    }


def matmul(left, right):
    return jnp.dot(left, right, preferred_element_type=jnp.float32)


def silu_slope(values):
    gate_value = jax.nn.sigmoid(values)
    return gate_value * (1.0 + values * (1.0 - gate_value))


def edge_tables(senders, receivers, send_table):
    extended = NODE_DEV + REGIONS * HALO
    owner_part = jnp.arange(EDGES, dtype=jnp.int32) // EDGE_DEV
    is_local = senders < NODE_DEV
    offset = jnp.maximum(senders - NODE_DEV, 0)
    source = offset // HALO
    slot_ids = offset % HALO
    entry = send_table[((source * REGIONS + owner_part) * HALO + slot_ids).astype(jnp.int32)]
    send_global = jnp.where(is_local, owner_part * NODE_DEV + senders, source * NODE_DEV + entry).astype(jnp.int32)
    recv_global = (owner_part * NODE_DEV + receivers).astype(jnp.int32)
    part_key = (owner_part * extended + senders).astype(jnp.int32)
    slot_part = jnp.arange(REGIONS * extended, dtype=jnp.int32) // extended
    slot_index = jnp.arange(REGIONS * extended, dtype=jnp.int32) % extended
    slot_offset = jnp.maximum(slot_index - NODE_DEV, 0)
    slot_source = slot_offset // HALO
    slot_entry = send_table[((slot_source * REGIONS + slot_part) * HALO + slot_offset % HALO).astype(jnp.int32)]
    remote_node = jnp.where(slot_entry >= 0, slot_source * NODE_DEV + slot_entry, NODES)
    slot_node = jnp.where(slot_index < NODE_DEV, slot_part * NODE_DEV + slot_index, remote_node).astype(jnp.int32)
    return send_global, recv_global, part_key, slot_node


def linearize(state_now, weights, send_global, recv_global):
    weight_send, weight_receive, weight_message, weight_node, weight_inbox, weight_output = weights
    pre_edge = matmul(state_now, weight_send)[send_global] + matmul(state_now, weight_receive)[recv_global]
    edge_act = jax.nn.silu(pre_edge).astype(jnp.bfloat16)
    edge_sum = jax.ops.segment_sum(edge_act.astype(jnp.float32), recv_global, num_segments=NODES).astype(jnp.bfloat16)
    inbox = matmul(edge_sum, weight_message).astype(jnp.bfloat16)
    pre_node = matmul(state_now, weight_node) + matmul(inbox, weight_inbox)
    return silu_slope(pre_edge), silu_slope(pre_node)


def reference(trajectory, increments, weight_send, weight_receive, weight_message, weight_node, weight_inbox, weight_output, senders, receivers, send_table):
    weights = (weight_send, weight_receive, weight_message, weight_node, weight_inbox, weight_output)
    send_global, recv_global, part_key, slot_node = edge_tables(senders, receivers, send_table)
    extended = NODE_DEV + REGIONS * HALO

    def tangent_step(pair):
        state_now, increment = pair
        edge_slope, node_slope = linearize(state_now, weights, send_global, recv_global)
        edge_pre = matmul(increment, weight_send)[send_global] + matmul(increment, weight_receive)[recv_global]
        edge_tangent = (edge_slope * edge_pre).astype(jnp.bfloat16)
        tangent_sum = jax.ops.segment_sum(edge_tangent.astype(jnp.float32), recv_global, num_segments=NODES).astype(jnp.bfloat16)
        inbox_tangent = matmul(tangent_sum, weight_message).astype(jnp.bfloat16)
        node_tangent = (node_slope * (matmul(increment, weight_node) + matmul(inbox_tangent, weight_inbox))).astype(jnp.bfloat16)
        return (increment.astype(jnp.float32) + matmul(node_tangent, weight_output)).astype(jnp.bfloat16)

    def adjoint_step(pair):
        state_now, cotangent = pair
        edge_slope, node_slope = linearize(state_now, weights, send_global, recv_global)
        node_bar = (node_slope * matmul(cotangent, weight_output.T)).astype(jnp.bfloat16)
        inbox_bar = matmul(node_bar, weight_inbox.T).astype(jnp.bfloat16)
        edge_bar = edge_slope * matmul(inbox_bar, weight_message.T)[recv_global]
        part_sums = jax.ops.segment_sum(edge_bar, part_key, num_segments=REGIONS * extended).astype(jnp.bfloat16)
        owned = jax.ops.segment_sum(part_sums.astype(jnp.float32), slot_node, num_segments=NODES + 1)[:NODES].astype(jnp.bfloat16)
        recv_sums = jax.ops.segment_sum(edge_bar, recv_global, num_segments=NODES).astype(jnp.bfloat16)
        total = cotangent.astype(jnp.float32) + matmul(node_bar, weight_node.T)
        return total + matmul(owned, weight_send.T) + matmul(recv_sums, weight_receive.T)

    tangents = lax.map(tangent_step, (trajectory, increments))
    before = jnp.concatenate([jnp.zeros_like(tangents[:1]), tangents[:-1]], axis=0)
    forward_image = (increments.astype(jnp.float32) - before.astype(jnp.float32)).astype(jnp.bfloat16)
    cotangents = jnp.concatenate([forward_image[1:], jnp.zeros_like(forward_image[:1])], axis=0)
    adjoints = lax.map(adjoint_step, (trajectory, cotangents))
    normal_image = (forward_image.astype(jnp.float32) - adjoints).astype(jnp.bfloat16)
    return forward_image, normal_image
```

```python
import jax
import jax.numpy as jnp
from jax import lax
from jax.experimental import pallas as pl
from jax.experimental.pallas import tpu as pltpu
from jax.sharding import PartitionSpec as P

MESH = pl.DeviceIdType.MESH
F32 = jnp.float32
BF16 = jnp.bfloat16

WIDTH = 512
OWN = 160
SLOT = 16
PARTS = 16
WINDOW = 16
HALO = PARTS * SLOT
EDGES = 1280
LANES = 128

AWAY = sorted(
    [(dy, dx) for dy in range(4) for dx in range(4) if dy or dx],
    key=lambda d: -(min(d[0], 4 - d[0]) + min(d[1], 4 - d[1])),
)
SEND, RECEIVE, MESSAGE, NODE, INBOX, OUTPUT = range(6)


def dot(left, right):
    return jnp.dot(left, right, preferred_element_type=F32)


def dot_t(left, right):
    return lax.dot_general(left, right, (((1,), (1,)), ((), ())), preferred_element_type=F32)


def sigmoid(values):
    return 0.5 * jnp.tanh(0.5 * values) + 0.5


def ones_where(mask):
    return jnp.where(mask, 1.0, 0.0).astype(BF16)


def down_rows(row):
    return jnp.broadcast_to(row.astype(F32), (LANES, LANES)).T


def kernel(
    x_hbm,
    v_hbm,
    ws_hbm,
    wr_hbm,
    wm_hbm,
    wn_hbm,
    wi_hbm,
    wo_hbm,
    snd_hbm,
    rcv_hbm,
    tab_hbm,
    fi_ref,
    ni_ref,
    xv,
    w,
    snd,
    rcv,
    tab,
    pick,
    pick_t,
    near,
    far,
    near_t,
    far_t,
    out_x,
    out_v,
    halo_x,
    halo_v,
    inc_next,
    tan_out,
    before,
    ret_out,
    ret_in,
    loc_x,
    loc_v,
    slope,
    act,
    load_sem,
    send_sem,
    recv_sem,
):
    me = lax.axis_index("mesh")
    k = lax.axis_index("tm")
    row, col = me // 4, lax.rem(me, 4)
    peers = [
        {"mesh": lax.rem(row + dy, 4) * 4 + lax.rem(col + dx, 4)} for dy, dx in AWAY
    ]
    after = {"tm": lax.rem(k + 1, WINDOW)}
    ahead = {"tm": lax.rem(k + WINDOW - 1, WINDOW)}

    barrier = pltpu.get_barrier_semaphore()
    for peer in peers + [after, ahead]:
        pl.semaphore_signal(barrier, inc=1, device_id=peer, device_id_type=MESH)

    loads = []
    pairs = [
        (tab_hbm, tab),
        (x_hbm.at[0], xv.at[pl.ds(0, OWN)]),
        (v_hbm.at[0], xv.at[pl.ds(OWN, OWN)]),
        (ws_hbm, w.at[SEND]),
        (snd_hbm, snd),
        (rcv_hbm, rcv),
        (wr_hbm, w.at[RECEIVE]),
        (wn_hbm, w.at[NODE]),
        (wm_hbm, w.at[MESSAGE]),
        (wi_hbm, w.at[INBOX]),
        (wo_hbm, w.at[OUTPUT]),
    ]
    for at, (src, dst) in enumerate(pairs):
        load = pltpu.make_async_copy(src, dst, load_sem.at[at])
        load.start()
        loads.append(load)

    loads[0].wait()
    lane = lax.broadcasted_iota(jnp.int32, (LANES, LANES), 1).astype(F32)
    for b in range(HALO // LANES):
        rows = pl.ds(b * LANES, LANES)
        column = down_rows(tab[b : b + 1, :])
        pick[rows, 0:LANES] = ones_where(column == lane)
        pick[rows, LANES:OWN] = ones_where(column[:, : OWN - LANES] == lane[:, : OWN - LANES] + LANES)
        pick_t[:, b * LANES : (b + 1) * LANES] = ones_where(
            jnp.broadcast_to(tab[b : b + 1, :], (OWN, LANES))
            == lax.broadcasted_iota(jnp.int32, (OWN, LANES), 0)
        )
    own_rows = pl.ds(pl.multiple_of(me * SLOT, SLOT), SLOT)
    nothing = jnp.zeros((SLOT, WIDTH), BF16)
    halo_x[own_rows, :] = nothing
    halo_v[own_rows, :] = nothing
    ret_in[own_rows, :] = nothing
    for load in loads[1:4]:
        load.wait()
    sent = dot(xv[...], w[SEND]).astype(BF16)
    out_x[...] = dot(pick[...], sent[:OWN]).astype(BF16)
    out_v[...] = dot(pick[...], sent[OWN:]).astype(BF16)

    def exchange(src, dst, at):
        for peer in peers:
            there = pl.ds(pl.multiple_of(peer["mesh"] * SLOT, SLOT), SLOT)
            pltpu.make_async_remote_copy(
                src_ref=src.at[there],
                dst_ref=dst.at[own_rows],
                send_sem=send_sem.at[at],
                recv_sem=recv_sem.at[at],
                device_id=peer,
                device_id_type=MESH,
            ).start()

    def whole(src, dst, at):
        rows = pl.ds(0, HALO - SLOT)
        return pltpu.make_async_remote_copy(
            src_ref=src.at[rows],
            dst_ref=dst.at[rows],
            send_sem=send_sem.at[at],
            recv_sem=recv_sem.at[at],
            device_id=peers[0],
            device_id_type=MESH,
        )

    pl.semaphore_wait(barrier, len(peers) + 2)
    exchange(out_x, halo_x, 0)
    exchange(out_v, halo_v, 1)
    to_ahead = pltpu.make_async_remote_copy(
        src_ref=xv.at[pl.ds(OWN, OWN)],
        dst_ref=inc_next,
        send_sem=send_sem.at[3],
        recv_sem=recv_sem.at[3],
        device_id=ahead,
        device_id_type=MESH,
    )
    to_ahead.start()

    loads[4].wait()
    loads[5].wait()
    for b in range(EDGES // LANES):
        rows = pl.ds(b * LANES, LANES)
        cols = slice(b * LANES, (b + 1) * LANES)
        s_row, r_row = snd[b : b + 1, :], rcv[b : b + 1, :]
        s_col, r_col = down_rows(s_row), down_rows(r_row) + OWN
        near[rows, 0:LANES] = ones_where(s_col == lane)
        near[rows, LANES : 2 * LANES] = ones_where(
            jnp.where(lane < OWN - LANES, s_col, r_col) == lane + LANES
        )
        near[rows, 2 * LANES : 2 * OWN] = ones_where(
            (r_col == lane + 2 * LANES)[:, : 2 * OWN - 2 * LANES]
        )
        far[rows, 0:LANES] = ones_where(s_col == lane + OWN)
        far[rows, LANES:HALO] = ones_where(s_col == lane + (OWN + LANES))
        place = lax.broadcasted_iota(jnp.int32, (OWN, LANES), 0)
        near_t[0:OWN, cols] = ones_where(jnp.broadcast_to(s_row, (OWN, LANES)) == place)
        near_t[OWN:, cols] = ones_where(jnp.broadcast_to(r_row, (OWN, LANES)) == place)
        far_t[:, cols] = ones_where(
            jnp.broadcast_to(s_row, (HALO, LANES))
            == lax.broadcasted_iota(jnp.int32, (HALO, LANES), 0) + OWN
        )

    loads[6].wait()
    received = dot(xv[...], w[RECEIVE]).astype(BF16)
    loc_x[...] = dot(near[...], jnp.concatenate([sent[:OWN], received[:OWN]], axis=0))
    loc_v[...] = dot(near[...], jnp.concatenate([sent[OWN:], received[OWN:]], axis=0))
    for load in loads[7:]:
        load.wait()
    node = dot(xv[...], w[NODE])
    w_mi = dot(w[MESSAGE], w[INBOX]).astype(BF16)
    w_oo = dot_t(w[OUTPUT], w[OUTPUT]).astype(BF16)

    whole(out_x, halo_x, 0).wait_recv()
    pre = loc_x[...] + dot(far[...], halo_x[...])
    gate = sigmoid(pre)
    gated = pre * gate
    act[...] = gated.astype(BF16)
    slope[...] = gate + gated * (1.0 - gate)
    edge_sum = dot(near_t[OWN:, :], act[...]).astype(BF16)
    pre_node = node[:OWN] + dot(edge_sum, w_mi)
    gate_node = sigmoid(pre_node)
    node_slope = gate_node + pre_node * gate_node * (1.0 - gate_node)

    to_ahead.wait_recv()
    increment = xv[OWN:, :].astype(F32)
    step = (inc_next[...].astype(F32) - increment).astype(BF16)
    step_bar = dot_t(step, w[OUTPUT])

    whole(out_v, halo_v, 1).wait_recv()
    act[...] = (slope[...] * (loc_v[...] + dot(far[...], halo_v[...]))).astype(BF16)
    tangent_sum = dot(near_t[OWN:, :], act[...]).astype(BF16)
    node_tangent = (node_slope * (node[OWN:] + dot(tangent_sum, w_mi))).astype(BF16)
    node_bar = node_slope * (step_bar - dot(node_tangent, w_oo))
    node_bar = jnp.where(k == WINDOW - 1, 0.0, node_bar).astype(BF16)
    edge_in = dot_t(node_bar, w_mi).astype(BF16)
    act[...] = (slope[...] * dot(near[:, OWN:], edge_in)).astype(BF16)
    ret_out[...] = dot(far_t[...], act[...]).astype(BF16)
    exchange(ret_out, ret_in, 2)

    tangent = (increment + dot(node_tangent, w[OUTPUT])).astype(BF16)
    tan_out[...] = tangent
    to_after = pltpu.make_async_remote_copy(
        src_ref=tan_out,
        dst_ref=before,
        send_sem=send_sem.at[4],
        recv_sem=recv_sem.at[4],
        device_id=after,
        device_id_type=MESH,
    )
    to_after.start()

    sums = dot(near_t[...], act[...])
    cotangent = (inc_next[...].astype(F32) - tangent.astype(F32)).astype(BF16).astype(F32)
    adjoint = jnp.where(k == WINDOW - 1, 0.0, cotangent)
    adjoint = adjoint + dot_t(node_bar, w[NODE]) + dot_t(sums[OWN:].astype(BF16), w[RECEIVE])

    to_after.wait_recv()
    shifted = jnp.where(k == 0, 0.0, before[...].astype(F32))
    forward = (increment - shifted).astype(BF16)
    fi_ref[0] = forward
    rest = forward.astype(F32) - adjoint

    whole(ret_out, ret_in, 2).wait_recv()
    owned = (sums[:OWN] + dot(pick_t[...], ret_in[...])).astype(BF16)
    ni_ref[0] = (rest - dot_t(owned, w[SEND])).astype(BF16)

    whole(out_x, halo_x, 0).wait_send()
    whole(out_v, halo_v, 1).wait_send()
    whole(ret_out, ret_in, 2).wait_send()
    to_ahead.wait_send()
    to_after.wait_send()


def on_device(
    trajectory,
    increments,
    weight_send,
    weight_receive,
    weight_message,
    weight_node,
    weight_inbox,
    weight_output,
    senders,
    receivers,
    send_table,
):
    block = jax.ShapeDtypeStruct((1, OWN, WIDTH), BF16)
    rows = lambda n: pltpu.VMEM((n, WIDTH), BF16)
    return pl.pallas_call(
        kernel,
        out_shape=(block, block),
        in_specs=[pl.BlockSpec(memory_space=pltpu.HBM)] * 11,
        out_specs=(pl.BlockSpec(memory_space=pltpu.VMEM),) * 2,
        scratch_shapes=[
            rows(2 * OWN),
            pltpu.VMEM((6, WIDTH, WIDTH), BF16),
            pltpu.VMEM((EDGES // LANES, LANES), jnp.int32),
            pltpu.VMEM((EDGES // LANES, LANES), jnp.int32),
            pltpu.VMEM((HALO // LANES, LANES), jnp.int32),
            pltpu.VMEM((HALO, OWN), BF16),
            pltpu.VMEM((OWN, HALO), BF16),
            pltpu.VMEM((EDGES, 2 * OWN), BF16),
            pltpu.VMEM((EDGES, HALO), BF16),
            pltpu.VMEM((2 * OWN, EDGES), BF16),
            pltpu.VMEM((HALO, EDGES), BF16),
            rows(HALO),
            rows(HALO),
            rows(HALO),
            rows(HALO),
            rows(OWN),
            rows(OWN),
            rows(OWN),
            rows(HALO),
            rows(HALO),
            pltpu.VMEM((EDGES, WIDTH), F32),
            pltpu.VMEM((EDGES, WIDTH), F32),
            pltpu.VMEM((EDGES, WIDTH), F32),
            pltpu.VMEM((EDGES, WIDTH), BF16),
            pltpu.SemaphoreType.DMA((11,)),
            pltpu.SemaphoreType.DMA((5,)),
            pltpu.SemaphoreType.DMA((5,)),
        ],
        compiler_params=pltpu.CompilerParams(
            collective_id=0, has_side_effects=True, vmem_limit_bytes=60 << 20
        ),
    )(
        trajectory,
        increments,
        weight_send,
        weight_receive,
        weight_message,
        weight_node,
        weight_inbox,
        weight_output,
        senders.reshape(EDGES // LANES, LANES),
        receivers.reshape(EDGES // LANES, LANES),
        send_table.reshape(HALO // LANES, LANES),
    )


def solution(mesh):
    nodes = P("tm", "mesh", None)
    in_specs = (nodes, nodes) + (P(),) * 6 + (P("mesh"),) * 3
    return jax.shard_map(
        on_device, mesh=mesh, in_specs=in_specs, out_specs=(nodes, nodes), check_vma=False
    )
```

```python
import jax
import jax.numpy as jnp
from jax import lax
from jax.experimental import pallas as pl
from jax.experimental.pallas import tpu as pltpu
from jax.sharding import PartitionSpec as P

MESH = pl.DeviceIdType.MESH
F32 = jnp.float32
BF16 = jnp.bfloat16

WIDTH = 512
OWN = 160
SLOT = 16
PARTS = 16
WINDOW = 16
HALO = PARTS * SLOT
EDGES = 1280
LANES = 128

AWAY = sorted(
    [(dy, dx) for dy in range(4) for dx in range(4) if dy or dx],
    key=lambda d: -(min(d[0], 4 - d[0]) + min(d[1], 4 - d[1])),
)
SEND, RECEIVE, MESSAGE, NODE, INBOX, OUTPUT = range(6)


def dot(left, right):
    return jnp.dot(left, right, preferred_element_type=F32)


def dot_t(left, right):
    return lax.dot_general(left, right, (((1,), (1,)), ((), ())), preferred_element_type=F32)


def sigmoid(values):
    return 0.5 * jnp.tanh(0.5 * values) + 0.5


def ones_where(mask):
    return jnp.where(mask, 1.0, 0.0).astype(BF16)


def down_rows(row):
    return jnp.broadcast_to(row.astype(F32), (LANES, LANES)).T


def kernel(
    x_hbm,
    v_hbm,
    ws_hbm,
    wr_hbm,
    wm_hbm,
    wn_hbm,
    wi_hbm,
    wo_hbm,
    snd_hbm,
    rcv_hbm,
    tab_hbm,
    fi_ref,
    ni_ref,
    xv,
    w,
    snd,
    rcv,
    tab,
    pick,
    pick_t,
    near,
    far,
    near_t,
    far_t,
    out_x,
    out_v,
    halo_x,
    halo_v,
    inc_next,
    tan_out,
    before,
    ret_out,
    ret_in,
    loc_x,
    loc_v,
    slope,
    act,
    load_sem,
    send_sem,
    recv_sem,
):
    me = lax.axis_index("mesh")
    k = lax.axis_index("tm")
    row, col = me // 4, lax.rem(me, 4)
    targets = [lax.rem(row + dy, 4) * 4 + lax.rem(col + dx, 4) for dy, dx in AWAY]
    sources = [lax.rem(row + 4 - dy, 4) * 4 + lax.rem(col + 4 - dx, 4) for dy, dx in AWAY]
    first, last = k == 0, k == WINDOW - 1
    after = {"tm": lax.rem(k + 1, WINDOW)}
    ahead = {"tm": lax.rem(k + WINDOW - 1, WINDOW)}

    barrier = pltpu.get_barrier_semaphore()

    def greet(peer):
        pl.semaphore_signal(barrier, inc=1, device_id=peer, device_id_type=MESH)

    for target in targets:
        greet({"mesh": target})
    pl.when(jnp.logical_not(last))(lambda: greet(after))
    pl.when(jnp.logical_not(first))(lambda: greet(ahead))
    greeted = len(AWAY) + 2 - first.astype(jnp.int32) - last.astype(jnp.int32)

    loads = []
    pairs = [
        (tab_hbm, tab),
        (x_hbm.at[0], xv.at[pl.ds(0, OWN)]),
        (v_hbm.at[0], xv.at[pl.ds(OWN, OWN)]),
        (ws_hbm, w.at[SEND]),
        (snd_hbm, snd),
        (rcv_hbm, rcv),
        (wr_hbm, w.at[RECEIVE]),
        (wn_hbm, w.at[NODE]),
        (wm_hbm, w.at[MESSAGE]),
        (wi_hbm, w.at[INBOX]),
        (wo_hbm, w.at[OUTPUT]),
    ]
    for at, (src, dst) in enumerate(pairs):
        load = pltpu.make_async_copy(src, dst, load_sem.at[at])
        load.start()
        loads.append(load)

    loads[0].wait()
    lane = lax.broadcasted_iota(jnp.int32, (LANES, LANES), 1).astype(F32)
    for b in range(HALO // LANES):
        rows = pl.ds(b * LANES, LANES)
        column = down_rows(tab[b : b + 1, :])
        pick[rows, 0:LANES] = ones_where(column == lane)
        pick[rows, LANES:OWN] = ones_where(column[:, : OWN - LANES] == lane[:, : OWN - LANES] + LANES)
        pick_t[:, b * LANES : (b + 1) * LANES] = ones_where(
            jnp.broadcast_to(tab[b : b + 1, :], (OWN, LANES))
            == lax.broadcasted_iota(jnp.int32, (OWN, LANES), 0)
        )
    own_rows = pl.ds(pl.multiple_of(me * SLOT, SLOT), SLOT)
    nothing = jnp.zeros((SLOT, WIDTH), BF16)
    halo_x[HALO - SLOT :, :] = nothing
    halo_v[HALO - SLOT :, :] = nothing
    ret_in[own_rows, :] = nothing

    @pl.when(first)
    def _():
        before[...] = jnp.zeros_like(before)

    @pl.when(last)
    def _():
        inc_next[...] = jnp.zeros_like(inc_next)

    for load in loads[1:4]:
        load.wait()
    sent = dot(xv[...], w[SEND]).astype(BF16)
    out_x[...] = dot(pick[...], sent[:OWN]).astype(BF16)
    out_v[...] = dot(pick[...], sent[OWN:]).astype(BF16)

    def send(src, dst, at, peer):
        pltpu.make_async_remote_copy(
            src_ref=src,
            dst_ref=dst,
            send_sem=send_sem.at[at],
            recv_sem=recv_sem.at[at],
            device_id=peer,
            device_id_type=MESH,
        ).start()

    def part(ref, p):
        return ref.at[pl.ds(pl.multiple_of(p * SLOT, SLOT), SLOT)]

    def block(ref, b):
        return ref.at[pl.ds(b * SLOT, SLOT)]

    def whole(src, dst, at):
        return pltpu.make_async_remote_copy(
            src_ref=src,
            dst_ref=dst,
            send_sem=send_sem.at[at],
            recv_sem=recv_sem.at[at],
            device_id={"mesh": targets[0]},
            device_id_type=MESH,
        )

    bulk = pl.ds(0, HALO - SLOT)
    all_x = whole(out_x.at[bulk], halo_x.at[bulk], 0)
    all_v = whole(out_v.at[bulk], halo_v.at[bulk], 1)
    all_back = whole(ret_out.at[bulk], ret_in.at[bulk], 2)
    all_inc = whole(xv.at[pl.ds(OWN, OWN)], inc_next, 3)
    all_tan = whole(tan_out, before, 4)

    pl.semaphore_wait(barrier, greeted)
    for src, dst, at in ((out_x, halo_x, 0), (out_v, halo_v, 1)):
        for b, target in enumerate(targets):
            send(part(src, target), block(dst, b), at, {"mesh": target})

    @pl.when(jnp.logical_not(first))
    def _():
        send(xv.at[pl.ds(OWN, OWN)], inc_next, 3, ahead)

    loads[4].wait()
    loads[5].wait()
    step16 = lax.broadcasted_iota(jnp.int32, (1, LANES), 1)
    far_keys = []
    for at in range(0, HALO, LANES):
        keys = jnp.full((1, LANES), -1, jnp.int32)
        for b in range(at // SLOT, min((at + LANES) // SLOT, len(AWAY))):
            inside = (step16 >= b * SLOT - at) & (step16 < (b + 1) * SLOT - at)
            keys = jnp.where(inside, step16 + (at - b * SLOT + OWN + sources[b] * SLOT), keys)
        far_keys.append(keys.astype(F32))
    for b in range(EDGES // LANES):
        rows = pl.ds(b * LANES, LANES)
        cols = slice(b * LANES, (b + 1) * LANES)
        s_row, r_row = snd[b : b + 1, :], rcv[b : b + 1, :]
        s_col, r_col = down_rows(s_row), down_rows(r_row) + OWN
        near[rows, 0:LANES] = ones_where(s_col == lane)
        near[rows, LANES : 2 * LANES] = ones_where(
            jnp.where(lane < OWN - LANES, s_col, r_col) == lane + LANES
        )
        near[rows, 2 * LANES : 2 * OWN] = ones_where(
            (r_col == lane + 2 * LANES)[:, : 2 * OWN - 2 * LANES]
        )
        for at, keys in enumerate(far_keys):
            far[rows, at * LANES : (at + 1) * LANES] = ones_where(s_col == keys)
        place = lax.broadcasted_iota(jnp.int32, (OWN, LANES), 0)
        near_t[0:OWN, cols] = ones_where(jnp.broadcast_to(s_row, (OWN, LANES)) == place)
        near_t[OWN:, cols] = ones_where(jnp.broadcast_to(r_row, (OWN, LANES)) == place)
        offset = jnp.broadcast_to(s_row, (SLOT, LANES)) - place[:SLOT] - OWN
        for at, source in enumerate(sources):
            far_t[at * SLOT : (at + 1) * SLOT, cols] = ones_where(offset == source * SLOT)
        far_t[HALO - SLOT :, cols] = jnp.zeros((SLOT, LANES), BF16)

    loads[6].wait()
    received = dot(xv[...], w[RECEIVE]).astype(BF16)
    loc_x[...] = dot(near[...], jnp.concatenate([sent[:OWN], received[:OWN]], axis=0))
    loc_v[...] = dot(near[...], jnp.concatenate([sent[OWN:], received[OWN:]], axis=0))
    for load in loads[7:]:
        load.wait()
    node = dot(xv[...], w[NODE])
    w_mi = dot(w[MESSAGE], w[INBOX]).astype(BF16)
    w_oo = dot_t(w[OUTPUT], w[OUTPUT]).astype(BF16)

    all_x.wait_recv()
    pre = loc_x[...] + dot(far[...], halo_x[...])
    gate = sigmoid(pre)
    gated = pre * gate
    act[...] = gated.astype(BF16)
    slope[...] = gate + gated * (1.0 - gate)
    edge_sum = dot(near_t[OWN:, :], act[...]).astype(BF16)
    pre_node = node[:OWN] + dot(edge_sum, w_mi)
    gate_node = sigmoid(pre_node)
    node_slope = gate_node + pre_node * gate_node * (1.0 - gate_node)

    pl.when(jnp.logical_not(last))(all_inc.wait_recv)
    increment = xv[OWN:, :].astype(F32)
    step = (inc_next[...].astype(F32) - increment).astype(BF16)
    step_bar = dot_t(step, w[OUTPUT])

    all_v.wait_recv()
    act[...] = (slope[...] * (loc_v[...] + dot(far[...], halo_v[...]))).astype(BF16)
    tangent_sum = dot(near_t[OWN:, :], act[...]).astype(BF16)
    node_tangent = (node_slope * (node[OWN:] + dot(tangent_sum, w_mi))).astype(BF16)
    node_bar = node_slope * (step_bar - dot(node_tangent, w_oo))
    node_bar = jnp.where(last, 0.0, node_bar).astype(BF16)
    edge_in = dot_t(node_bar, w_mi).astype(BF16)
    act[...] = (slope[...] * dot(near[:, OWN:], edge_in)).astype(BF16)
    half = HALO // 2
    for at in (0, half):
        ret_out[at : at + half, :] = dot(far_t[at : at + half, :], act[...]).astype(BF16)
        for b in range(at // SLOT, min((at + half) // SLOT, len(AWAY))):
            send(block(ret_out, b), part(ret_in, me), 2, {"mesh": sources[b]})

    tangent = (increment + dot(node_tangent, w[OUTPUT])).astype(BF16)
    tan_out[...] = tangent

    @pl.when(jnp.logical_not(last))
    def _():
        send(tan_out, before, 4, after)

    sums = dot(near_t[...], act[...])
    cotangent = (inc_next[...].astype(F32) - tangent.astype(F32)).astype(BF16).astype(F32)
    adjoint = jnp.where(last, 0.0, cotangent)
    adjoint = adjoint + dot_t(node_bar, w[NODE]) + dot_t(sums[OWN:].astype(BF16), w[RECEIVE])

    pl.when(jnp.logical_not(first))(all_tan.wait_recv)
    forward = (increment - before[...].astype(F32)).astype(BF16)
    fi_ref[0] = forward
    rest = forward.astype(F32) - adjoint

    all_back.wait_recv()
    owned = (sums[:OWN] + dot(pick_t[...], ret_in[...])).astype(BF16)
    ni_ref[0] = (rest - dot_t(owned, w[SEND])).astype(BF16)

    all_x.wait_send()
    all_v.wait_send()
    all_back.wait_send()
    pl.when(jnp.logical_not(first))(all_inc.wait_send)
    pl.when(jnp.logical_not(last))(all_tan.wait_send)


def store(fi_vmem, ni_vmem, fi_hbm, ni_hbm, sem):
    copies = [
        pltpu.make_async_copy(fi_vmem, fi_hbm, sem.at[0]),
        pltpu.make_async_copy(ni_vmem, ni_hbm, sem.at[1]),
    ]
    for copy in copies:
        copy.start()
    for copy in copies:
        copy.wait()


def on_device(
    trajectory,
    increments,
    weight_send,
    weight_receive,
    weight_message,
    weight_node,
    weight_inbox,
    weight_output,
    senders,
    receivers,
    send_table,
):
    image = jax.ShapeDtypeStruct((1, OWN, WIDTH), BF16)
    rows = lambda n: pltpu.VMEM((n, WIDTH), BF16)
    operands = (
        trajectory,
        increments,
        weight_send,
        weight_receive,
        weight_message,
        weight_node,
        weight_inbox,
        weight_output,
        senders.reshape(EDGES // LANES, LANES),
        receivers.reshape(EDGES // LANES, LANES),
        send_table.reshape(HALO // LANES, LANES),
    )
    images = pl.pallas_call(
        kernel,
        out_shape=(pltpu.VMEM(image.shape, BF16),) * 2,
        in_specs=[pl.BlockSpec(memory_space=pl.ANY)] * 11,
        out_specs=(pl.BlockSpec(memory_space=pltpu.VMEM),) * 2,
        scratch_shapes=[
            rows(2 * OWN),
            pltpu.VMEM((6, WIDTH, WIDTH), BF16),
            pltpu.VMEM((EDGES // LANES, LANES), jnp.int32),
            pltpu.VMEM((EDGES // LANES, LANES), jnp.int32),
            pltpu.VMEM((HALO // LANES, LANES), jnp.int32),
            pltpu.VMEM((HALO, OWN), BF16),
            pltpu.VMEM((OWN, HALO), BF16),
            pltpu.VMEM((EDGES, 2 * OWN), BF16),
            pltpu.VMEM((EDGES, HALO), BF16),
            pltpu.VMEM((2 * OWN, EDGES), BF16),
            pltpu.VMEM((HALO, EDGES), BF16),
            rows(HALO),
            rows(HALO),
            rows(HALO),
            rows(HALO),
            rows(OWN),
            rows(OWN),
            rows(OWN),
            rows(HALO),
            rows(HALO),
            pltpu.VMEM((EDGES, WIDTH), F32),
            pltpu.VMEM((EDGES, WIDTH), F32),
            pltpu.VMEM((EDGES, WIDTH), F32),
            pltpu.VMEM((EDGES, WIDTH), BF16),
            pltpu.SemaphoreType.DMA((11,)),
            pltpu.SemaphoreType.DMA((5,)),
            pltpu.SemaphoreType.DMA((5,)),
        ],
        compiler_params=pltpu.CompilerParams(
            collective_id=0, has_side_effects=True, vmem_limit_bytes=40 << 20
        ),
    )(*[pltpu.with_memory_space_constraint(operand, pltpu.HBM) for operand in operands])
    return pl.pallas_call(
        store,
        out_shape=(image, image),
        in_specs=[pl.BlockSpec(memory_space=pltpu.VMEM)] * 2,
        out_specs=(pl.BlockSpec(memory_space=pl.ANY),) * 2,
        scratch_shapes=[pltpu.SemaphoreType.DMA((2,))],
        compiler_params=pltpu.CompilerParams(vmem_limit_bytes=4 << 20),
    )(*images)


def solution(mesh):
    nodes = P("tm", "mesh", None)
    in_specs = (nodes, nodes) + (P(),) * 6 + (P("mesh"),) * 3
    return jax.shard_map(
        on_device, mesh=mesh, in_specs=in_specs, out_specs=(nodes, nodes), check_vma=False
    )
```

```python
import jax
import jax.numpy as jnp
from jax import lax
from jax.experimental import pallas as pl
from jax.experimental.pallas import tpu as pltpu
from jax.sharding import PartitionSpec as P

MESH = pl.DeviceIdType.MESH
F32 = jnp.float32
BF16 = jnp.bfloat16

WIDTH = 512
OWN = 160
SLOT = 16
PARTS = 16
WINDOW = 16
HALO = PARTS * SLOT
EDGES = 1280
LANES = 128

AWAY = sorted(
    [(dy, dx) for dy in range(4) for dx in range(4) if dy or dx],
    key=lambda d: -(min(d[0], 4 - d[0]) + min(d[1], 4 - d[1])),
)
SEND, RECEIVE, MESSAGE, NODE, INBOX, OUTPUT = range(6)


def dot(left, right):
    return jnp.dot(left, right, preferred_element_type=F32)


def dot_t(left, right):
    return lax.dot_general(left, right, (((1,), (1,)), ((), ())), preferred_element_type=F32)


def sigmoid(values):
    return 0.5 * jnp.tanh(0.5 * values) + 0.5


def ones_where(mask):
    return jnp.where(mask, 1.0, 0.0).astype(BF16)


def down_rows(row):
    return jnp.broadcast_to(row.astype(F32), (LANES, LANES)).T


def kernel(
    x_hbm,
    v_hbm,
    ws_hbm,
    wr_hbm,
    wm_hbm,
    wn_hbm,
    wi_hbm,
    wo_hbm,
    snd_hbm,
    rcv_hbm,
    tab_hbm,
    fi_ref,
    ni_ref,
    xv,
    w,
    ends,
    tab,
    pick,
    pick_t,
    near,
    far,
    near_t,
    far_t,
    out_x,
    out_v,
    halo_x,
    halo_v,
    inc_next,
    tan_out,
    before,
    ret_out,
    ret_in,
    loc_x,
    loc_v,
    slope,
    act,
    load_sem,
    send_sem,
    recv_sem,
):
    me = lax.axis_index("mesh")
    k = lax.axis_index("tm")
    row, col = me // 4, lax.rem(me, 4)
    targets = [lax.rem(row + dy, 4) * 4 + lax.rem(col + dx, 4) for dy, dx in AWAY]
    sources = [lax.rem(row + 4 - dy, 4) * 4 + lax.rem(col + 4 - dx, 4) for dy, dx in AWAY]
    first, last = k == 0, k == WINDOW - 1
    after = {"tm": lax.rem(k + 1, WINDOW)}
    ahead = {"tm": lax.rem(k + WINDOW - 1, WINDOW)}

    barrier = pltpu.get_barrier_semaphore()

    def greet(peer):
        pl.semaphore_signal(barrier, inc=1, device_id=peer, device_id_type=MESH)

    for target in targets:
        greet({"mesh": target})
    pl.when(jnp.logical_not(last))(lambda: greet(after))
    pl.when(jnp.logical_not(first))(lambda: greet(ahead))
    greeted = len(AWAY) + 2 - first.astype(jnp.int32) - last.astype(jnp.int32)

    groups = [
        (tab, [(tab_hbm, tab)]),
        (xv, [(x_hbm.at[0], xv.at[pl.ds(0, OWN)]), (v_hbm.at[0], xv.at[pl.ds(OWN, OWN)])]),
        (w.at[SEND], [(ws_hbm, w.at[SEND])]),
        (ends, [(snd_hbm, ends.at[0]), (rcv_hbm, ends.at[1])]),
        (w.at[RECEIVE], [(wr_hbm, w.at[RECEIVE])]),
        (
            w.at[pl.ds(MESSAGE, 4)],
            [
                (hbm, w.at[at])
                for at, hbm in ((NODE, wn_hbm), (MESSAGE, wm_hbm), (INBOX, wi_hbm), (OUTPUT, wo_hbm))
            ],
        ),
    ]
    loads = []
    for at, (whole_group, pairs) in enumerate(groups):
        for src, dst in pairs:
            pltpu.make_async_copy(src, dst, load_sem.at[at]).start()
        loads.append(pltpu.make_async_copy(whole_group, whole_group, load_sem.at[at]))

    loads[0].wait()
    lane = lax.broadcasted_iota(jnp.int32, (LANES, LANES), 1).astype(F32)
    for b in range(HALO // LANES):
        rows = pl.ds(b * LANES, LANES)
        column = down_rows(tab[b : b + 1, :])
        pick[rows, 0:LANES] = ones_where(column == lane)
        pick[rows, LANES:OWN] = ones_where(column[:, : OWN - LANES] == lane[:, : OWN - LANES] + LANES)
        pick_t[:, b * LANES : (b + 1) * LANES] = ones_where(
            jnp.broadcast_to(tab[b : b + 1, :], (OWN, LANES))
            == lax.broadcasted_iota(jnp.int32, (OWN, LANES), 0)
        )
    own_rows = pl.ds(pl.multiple_of(me * SLOT, SLOT), SLOT)
    nothing = jnp.zeros((SLOT, WIDTH), BF16)
    halo_x[HALO - SLOT :, :] = nothing
    halo_v[HALO - SLOT :, :] = nothing
    ret_in[own_rows, :] = nothing

    @pl.when(first)
    def _():
        before[...] = jnp.zeros_like(before)

    @pl.when(last)
    def _():
        inc_next[...] = jnp.zeros_like(inc_next)

    loads[1].wait()
    loads[2].wait()
    sent = dot(xv[...], w[SEND]).astype(BF16)
    out_x[...] = dot(pick[...], sent[:OWN]).astype(BF16)
    out_v[...] = dot(pick[...], sent[OWN:]).astype(BF16)

    def send(src, dst, at, peer):
        pltpu.make_async_remote_copy(
            src_ref=src,
            dst_ref=dst,
            send_sem=send_sem.at[at],
            recv_sem=recv_sem.at[at],
            device_id=peer,
            device_id_type=MESH,
        ).start()

    def part(ref, p):
        return ref.at[pl.ds(pl.multiple_of(p * SLOT, SLOT), SLOT)]

    def block(ref, b):
        return ref.at[pl.ds(b * SLOT, SLOT)]

    def whole(src, dst, at):
        return pltpu.make_async_remote_copy(
            src_ref=src,
            dst_ref=dst,
            send_sem=send_sem.at[at],
            recv_sem=recv_sem.at[at],
            device_id={"mesh": targets[0]},
            device_id_type=MESH,
        )

    bulk = pl.ds(0, HALO - SLOT)
    all_x = whole(out_x.at[bulk], halo_x.at[bulk], 0)
    all_v = whole(out_v.at[bulk], halo_v.at[bulk], 1)
    all_back = whole(ret_out.at[bulk], ret_in.at[bulk], 2)
    all_inc = whole(xv.at[pl.ds(OWN, OWN)], inc_next, 3)
    all_tan = whole(tan_out, before, 4)

    pl.semaphore_wait(barrier, greeted)
    for src, dst, at in ((out_x, halo_x, 0), (out_v, halo_v, 1)):
        for b, target in enumerate(targets):
            send(part(src, target), block(dst, b), at, {"mesh": target})

    @pl.when(jnp.logical_not(first))
    def _():
        send(xv.at[pl.ds(OWN, OWN)], inc_next, 3, ahead)

    loads[3].wait()
    step16 = lax.broadcasted_iota(jnp.int32, (1, LANES), 1)
    far_keys = []
    for at in range(0, HALO, LANES):
        keys = jnp.full((1, LANES), -1, jnp.int32)
        for b in range(at // SLOT, min((at + LANES) // SLOT, len(AWAY))):
            inside = (step16 >= b * SLOT - at) & (step16 < (b + 1) * SLOT - at)
            keys = jnp.where(inside, step16 + (at - b * SLOT + OWN + sources[b] * SLOT), keys)
        far_keys.append(keys.astype(F32))
    for b in range(EDGES // LANES):
        rows = pl.ds(b * LANES, LANES)
        cols = slice(b * LANES, (b + 1) * LANES)
        s_row, r_row = ends[0, b : b + 1, :], ends[1, b : b + 1, :]
        s_col, r_col = down_rows(s_row), down_rows(r_row) + OWN
        near[rows, 0:LANES] = ones_where(s_col == lane)
        near[rows, LANES : 2 * LANES] = ones_where(
            jnp.where(lane < OWN - LANES, s_col, r_col) == lane + LANES
        )
        near[rows, 2 * LANES : 2 * OWN] = ones_where(
            (r_col == lane + 2 * LANES)[:, : 2 * OWN - 2 * LANES]
        )
        for at, keys in enumerate(far_keys):
            far[rows, at * LANES : (at + 1) * LANES] = ones_where(s_col == keys)
        place = lax.broadcasted_iota(jnp.int32, (OWN, LANES), 0)
        near_t[0:OWN, cols] = ones_where(jnp.broadcast_to(s_row, (OWN, LANES)) == place)
        near_t[OWN:, cols] = ones_where(jnp.broadcast_to(r_row, (OWN, LANES)) == place)
        offset = jnp.broadcast_to(s_row, (SLOT, LANES)) - place[:SLOT] - OWN
        for at, source in enumerate(sources):
            far_t[at * SLOT : (at + 1) * SLOT, cols] = ones_where(offset == source * SLOT)
        far_t[HALO - SLOT :, cols] = jnp.zeros((SLOT, LANES), BF16)

    loads[4].wait()
    received = dot(xv[...], w[RECEIVE]).astype(BF16)
    loc_x[...] = dot(near[...], jnp.concatenate([sent[:OWN], received[:OWN]], axis=0))
    loc_v[...] = dot(near[...], jnp.concatenate([sent[OWN:], received[OWN:]], axis=0))
    loads[5].wait()
    node = dot(xv[...], w[NODE])
    w_mi = dot(w[MESSAGE], w[INBOX]).astype(BF16)
    w_oo = dot_t(w[OUTPUT], w[OUTPUT]).astype(BF16)

    all_x.wait_recv()
    pre = loc_x[...] + dot(far[...], halo_x[...])
    gate = sigmoid(pre)
    gated = pre * gate
    act[...] = gated.astype(BF16)
    slope[...] = gate + gated * (1.0 - gate)
    edge_sum = dot(near_t[OWN:, :], act[...]).astype(BF16)
    pre_node = node[:OWN] + dot(edge_sum, w_mi)
    gate_node = sigmoid(pre_node)
    node_slope = gate_node + pre_node * gate_node * (1.0 - gate_node)

    pl.when(jnp.logical_not(last))(all_inc.wait_recv)
    increment = xv[OWN:, :].astype(F32)
    step = (inc_next[...].astype(F32) - increment).astype(BF16)
    step_bar = dot_t(step, w[OUTPUT])

    all_v.wait_recv()
    act[...] = (slope[...] * (loc_v[...] + dot(far[...], halo_v[...]))).astype(BF16)
    tangent_sum = dot(near_t[OWN:, :], act[...]).astype(BF16)
    node_tangent = (node_slope * (node[OWN:] + dot(tangent_sum, w_mi))).astype(BF16)
    node_bar = node_slope * (step_bar - dot(node_tangent, w_oo))
    node_bar = jnp.where(last, 0.0, node_bar).astype(BF16)
    edge_in = dot_t(node_bar, w_mi).astype(BF16)
    act[...] = (slope[...] * dot(near[:, OWN:], edge_in)).astype(BF16)
    half = HALO // 2
    for at in (half, 0):
        ret_out[at : at + half, :] = dot(far_t[at : at + half, :], act[...]).astype(BF16)
        for b in range(at // SLOT, min((at + half) // SLOT, len(AWAY))):
            send(block(ret_out, b), part(ret_in, me), 2, {"mesh": sources[b]})

    tangent = (increment + dot(node_tangent, w[OUTPUT])).astype(BF16)
    tan_out[...] = tangent

    @pl.when(jnp.logical_not(last))
    def _():
        send(tan_out, before, 4, after)

    sums = dot(near_t[...], act[...])
    cotangent = (inc_next[...].astype(F32) - tangent.astype(F32)).astype(BF16).astype(F32)
    adjoint = jnp.where(last, 0.0, cotangent)
    adjoint = adjoint + dot_t(node_bar, w[NODE]) + dot_t(sums[OWN:].astype(BF16), w[RECEIVE])

    pl.when(jnp.logical_not(first))(all_tan.wait_recv)
    forward = (increment - before[...].astype(F32)).astype(BF16)
    fi_ref[0] = forward
    rest = forward.astype(F32) - adjoint

    all_back.wait_recv()
    owned = (sums[:OWN] + dot(pick_t[...], ret_in[...])).astype(BF16)
    ni_ref[0] = (rest - dot_t(owned, w[SEND])).astype(BF16)

    all_x.wait_send()
    all_v.wait_send()
    all_back.wait_send()
    pl.when(jnp.logical_not(first))(all_inc.wait_send)
    pl.when(jnp.logical_not(last))(all_tan.wait_send)


def store(fi_vmem, ni_vmem, fi_hbm, ni_hbm, sem):
    copies = [
        pltpu.make_async_copy(fi_vmem, fi_hbm, sem.at[0]),
        pltpu.make_async_copy(ni_vmem, ni_hbm, sem.at[1]),
    ]
    for copy in copies:
        copy.start()
    for copy in copies:
        copy.wait()


def on_device(
    trajectory,
    increments,
    weight_send,
    weight_receive,
    weight_message,
    weight_node,
    weight_inbox,
    weight_output,
    senders,
    receivers,
    send_table,
):
    image = jax.ShapeDtypeStruct((1, OWN, WIDTH), BF16)
    rows = lambda n: pltpu.VMEM((n, WIDTH), BF16)
    operands = (
        trajectory,
        increments,
        weight_send,
        weight_receive,
        weight_message,
        weight_node,
        weight_inbox,
        weight_output,
        senders.reshape(EDGES // LANES, LANES),
        receivers.reshape(EDGES // LANES, LANES),
        send_table.reshape(HALO // LANES, LANES),
    )
    images = pl.pallas_call(
        kernel,
        out_shape=(pltpu.VMEM(image.shape, BF16),) * 2,
        in_specs=[pl.BlockSpec(memory_space=pl.ANY)] * 11,
        out_specs=(pl.BlockSpec(memory_space=pltpu.VMEM),) * 2,
        scratch_shapes=[
            rows(2 * OWN),
            pltpu.VMEM((6, WIDTH, WIDTH), BF16),
            pltpu.VMEM((2, EDGES // LANES, LANES), jnp.int32),
            pltpu.VMEM((HALO // LANES, LANES), jnp.int32),
            pltpu.VMEM((HALO, OWN), BF16),
            pltpu.VMEM((OWN, HALO), BF16),
            pltpu.VMEM((EDGES, 2 * OWN), BF16),
            pltpu.VMEM((EDGES, HALO), BF16),
            pltpu.VMEM((2 * OWN, EDGES), BF16),
            pltpu.VMEM((HALO, EDGES), BF16),
            rows(HALO),
            rows(HALO),
            rows(HALO),
            rows(HALO),
            rows(OWN),
            rows(OWN),
            rows(OWN),
            rows(HALO),
            rows(HALO),
            pltpu.VMEM((EDGES, WIDTH), F32),
            pltpu.VMEM((EDGES, WIDTH), F32),
            pltpu.VMEM((EDGES, WIDTH), F32),
            pltpu.VMEM((EDGES, WIDTH), BF16),
            pltpu.SemaphoreType.DMA((6,)),
            pltpu.SemaphoreType.DMA((5,)),
            pltpu.SemaphoreType.DMA((5,)),
        ],
        compiler_params=pltpu.CompilerParams(
            collective_id=0, has_side_effects=True, vmem_limit_bytes=40 << 20
        ),
    )(*[pltpu.with_memory_space_constraint(operand, pltpu.HBM) for operand in operands])
    return pl.pallas_call(
        store,
        out_shape=(image, image),
        in_specs=[pl.BlockSpec(memory_space=pltpu.VMEM)] * 2,
        out_specs=(pl.BlockSpec(memory_space=pl.ANY),) * 2,
        scratch_shapes=[pltpu.SemaphoreType.DMA((2,))],
        compiler_params=pltpu.CompilerParams(vmem_limit_bytes=4 << 20),
    )(*images)


def solution(mesh):
    nodes = P("tm", "mesh", None)
    in_specs = (nodes, nodes) + (P(),) * 6 + (P("mesh"),) * 3
    return jax.shard_map(
        on_device, mesh=mesh, in_specs=in_specs, out_specs=(nodes, nodes), check_vma=False
    )
```

```python
import jax
import jax.numpy as jnp
from jax import lax
from jax.experimental import pallas as pl
from jax.experimental.pallas import tpu as pltpu
from jax.sharding import PartitionSpec as P

MESH = pl.DeviceIdType.MESH
F32 = jnp.float32
BF16 = jnp.bfloat16

WIDTH = 512
OWN = 160
SLOT = 16
PARTS = 16
WINDOW = 16
HALO = PARTS * SLOT
EDGES = 1280
LANES = 128

AWAY = sorted(
    [(dy, dx) for dy in range(4) for dx in range(4) if dy or dx],
    key=lambda d: -(min(d[0], 4 - d[0]) + min(d[1], 4 - d[1])),
)
SEND, RECEIVE, MESSAGE, NODE, INBOX, OUTPUT = range(6)


def dot(left, right):
    return jnp.dot(left, right, preferred_element_type=F32)


def dot_t(left, right):
    return lax.dot_general(left, right, (((1,), (1,)), ((), ())), preferred_element_type=F32)


def sigmoid(values):
    return 0.5 * jnp.tanh(0.5 * values) + 0.5


def ones_where(mask):
    return jnp.where(mask, 1.0, 0.0).astype(BF16)


def down_rows(row):
    return jnp.broadcast_to(row.astype(F32), (LANES, LANES)).T


def kernel(
    x_hbm,
    v_hbm,
    ws_hbm,
    wr_hbm,
    wm_hbm,
    wn_hbm,
    wi_hbm,
    wo_hbm,
    snd_hbm,
    rcv_hbm,
    tab_hbm,
    fi_ref,
    ni_ref,
    xv,
    w,
    ends,
    tab,
    pick,
    pick_t,
    near,
    far,
    near_t,
    far_t,
    out_x,
    out_v,
    halo_x,
    halo_v,
    inc_next,
    tan_out,
    before,
    ret_out,
    ret_in,
    loc_x,
    loc_v,
    slope,
    act,
    turned,
    load_sem,
    send_sem,
    recv_sem,
):
    me = lax.axis_index("mesh")
    k = lax.axis_index("tm")
    row, col = me // 4, lax.rem(me, 4)
    targets = [lax.rem(row + dy, 4) * 4 + lax.rem(col + dx, 4) for dy, dx in AWAY]
    sources = [lax.rem(row + 4 - dy, 4) * 4 + lax.rem(col + 4 - dx, 4) for dy, dx in AWAY]
    first, last = k == 0, k == WINDOW - 1
    after = {"tm": lax.rem(k + 1, WINDOW)}
    ahead = {"tm": lax.rem(k + WINDOW - 1, WINDOW)}

    barrier = pltpu.get_barrier_semaphore()

    def greet(peer):
        pl.semaphore_signal(barrier, inc=1, device_id=peer, device_id_type=MESH)

    for target in targets:
        greet({"mesh": target})
    pl.when(jnp.logical_not(last))(lambda: greet(after))
    pl.when(jnp.logical_not(first))(lambda: greet(ahead))
    greeted = len(AWAY) + 2 - first.astype(jnp.int32) - last.astype(jnp.int32)

    groups = [
        (tab, [(tab_hbm, tab)]),
        (xv, [(x_hbm.at[0], xv.at[pl.ds(0, OWN)]), (v_hbm.at[0], xv.at[pl.ds(OWN, OWN)])]),
        (w.at[SEND], [(ws_hbm, w.at[SEND])]),
        (ends, [(snd_hbm, ends.at[0]), (rcv_hbm, ends.at[1])]),
        (w.at[RECEIVE], [(wr_hbm, w.at[RECEIVE])]),
        (
            w.at[pl.ds(MESSAGE, 4)],
            [
                (hbm, w.at[at])
                for at, hbm in ((NODE, wn_hbm), (MESSAGE, wm_hbm), (INBOX, wi_hbm), (OUTPUT, wo_hbm))
            ],
        ),
    ]
    loads = []
    for at, (whole_group, pairs) in enumerate(groups):
        for src, dst in pairs:
            pltpu.make_async_copy(src, dst, load_sem.at[at]).start()
        loads.append(pltpu.make_async_copy(whole_group, whole_group, load_sem.at[at]))

    loads[0].wait()
    lane = lax.broadcasted_iota(jnp.int32, (LANES, LANES), 1).astype(F32)
    for b in range(HALO // LANES):
        rows = pl.ds(b * LANES, LANES)
        column = down_rows(tab[b : b + 1, :])
        pick[rows, 0:LANES] = ones_where(column == lane)
        pick[rows, LANES:OWN] = ones_where(column[:, : OWN - LANES] == lane[:, : OWN - LANES] + LANES)
        pick_t[:, b * LANES : (b + 1) * LANES] = ones_where(
            jnp.broadcast_to(tab[b : b + 1, :], (OWN, LANES))
            == lax.broadcasted_iota(jnp.int32, (OWN, LANES), 0)
        )
    own_rows = pl.ds(pl.multiple_of(me * SLOT, SLOT), SLOT)
    nothing = jnp.zeros((SLOT, WIDTH), BF16)
    halo_x[HALO - SLOT :, :] = nothing
    halo_v[HALO - SLOT :, :] = nothing
    ret_in[own_rows, :] = nothing

    @pl.when(first)
    def _():
        before[...] = jnp.zeros_like(before)

    @pl.when(last)
    def _():
        inc_next[...] = jnp.zeros_like(inc_next)

    loads[1].wait()
    loads[2].wait()
    sent = dot(xv[...], w[SEND]).astype(BF16)
    out_x[...] = dot(pick[...], sent[:OWN]).astype(BF16)
    out_v[...] = dot(pick[...], sent[OWN:]).astype(BF16)

    def send(src, dst, at, peer):
        pltpu.make_async_remote_copy(
            src_ref=src,
            dst_ref=dst,
            send_sem=send_sem.at[at],
            recv_sem=recv_sem.at[at],
            device_id=peer,
            device_id_type=MESH,
        ).start()

    def part(ref, p):
        return ref.at[pl.ds(pl.multiple_of(p * SLOT, SLOT), SLOT)]

    def block(ref, b):
        return ref.at[pl.ds(b * SLOT, SLOT)]

    def whole(src, dst, at):
        return pltpu.make_async_remote_copy(
            src_ref=src,
            dst_ref=dst,
            send_sem=send_sem.at[at],
            recv_sem=recv_sem.at[at],
            device_id={"mesh": targets[0]},
            device_id_type=MESH,
        )

    bulk = pl.ds(0, HALO - SLOT)
    all_x = whole(out_x.at[bulk], halo_x.at[bulk], 0)
    all_v = whole(out_v.at[bulk], halo_v.at[bulk], 1)
    all_back = whole(ret_out.at[bulk], ret_in.at[bulk], 2)
    all_inc = whole(xv.at[pl.ds(OWN, OWN)], inc_next, 3)
    all_tan = whole(tan_out, before, 4)

    pl.semaphore_wait(barrier, greeted)
    for src, dst, at in ((out_x, halo_x, 0), (out_v, halo_v, 1)):
        for b, target in enumerate(targets):
            send(part(src, target), block(dst, b), at, {"mesh": target})

    @pl.when(jnp.logical_not(first))
    def _():
        send(xv.at[pl.ds(OWN, OWN)], inc_next, 3, ahead)

    loads[3].wait()
    step16 = lax.broadcasted_iota(jnp.int32, (1, LANES), 1)
    far_keys = []
    for at in range(0, HALO, LANES):
        keys = jnp.full((1, LANES), -1, jnp.int32)
        for b in range(at // SLOT, min((at + LANES) // SLOT, len(AWAY))):
            inside = (step16 >= b * SLOT - at) & (step16 < (b + 1) * SLOT - at)
            keys = jnp.where(inside, step16 + (at - b * SLOT + OWN + sources[b] * SLOT), keys)
        far_keys.append(keys.astype(F32))
    for b in range(EDGES // LANES):
        rows = pl.ds(b * LANES, LANES)
        cols = slice(b * LANES, (b + 1) * LANES)
        s_row, r_row = ends[0, b : b + 1, :], ends[1, b : b + 1, :]
        s_col, r_col = down_rows(s_row), down_rows(r_row) + OWN
        near[rows, 0:LANES] = ones_where(s_col == lane)
        near[rows, LANES : 2 * LANES] = ones_where(
            jnp.where(lane < OWN - LANES, s_col, r_col) == lane + LANES
        )
        near[rows, 2 * LANES : 2 * OWN] = ones_where(
            (r_col == lane + 2 * LANES)[:, : 2 * OWN - 2 * LANES]
        )
        for at, keys in enumerate(far_keys):
            far[rows, at * LANES : (at + 1) * LANES] = ones_where(s_col == keys)
        place = lax.broadcasted_iota(jnp.int32, (OWN, LANES), 0)
        near_t[0:OWN, cols] = ones_where(jnp.broadcast_to(s_row, (OWN, LANES)) == place)
        near_t[OWN:, cols] = ones_where(jnp.broadcast_to(r_row, (OWN, LANES)) == place)
        offset = jnp.broadcast_to(s_row, (SLOT, LANES)) - place[:SLOT] - OWN
        for at, source in enumerate(sources):
            far_t[at * SLOT : (at + 1) * SLOT, cols] = ones_where(offset == source * SLOT)
        far_t[HALO - SLOT :, cols] = jnp.zeros((SLOT, LANES), BF16)

    loads[4].wait()
    received = dot(xv[...], w[RECEIVE]).astype(BF16)
    loc_x[...] = dot(near[...], jnp.concatenate([sent[:OWN], received[:OWN]], axis=0))
    loc_v[...] = dot(near[...], jnp.concatenate([sent[OWN:], received[OWN:]], axis=0))
    loads[5].wait()
    node = dot(xv[...], w[NODE])
    w_mi = dot(w[MESSAGE], w[INBOX]).astype(BF16)
    turned[0] = w_mi.T
    turned[1] = w[SEND].T
    w_oo = dot_t(w[OUTPUT], w[OUTPUT]).astype(BF16)

    all_x.wait_recv()
    pre = loc_x[...] + dot(far[...], halo_x[...])
    gate = sigmoid(pre)
    gated = pre * gate
    act[...] = gated.astype(BF16)
    slope[...] = gate + gated * (1.0 - gate)
    edge_sum = dot(near_t[OWN:, :], act[...]).astype(BF16)
    pre_node = node[:OWN] + dot(edge_sum, w_mi)
    gate_node = sigmoid(pre_node)
    node_slope = gate_node + pre_node * gate_node * (1.0 - gate_node)

    pl.when(jnp.logical_not(last))(all_inc.wait_recv)
    increment = xv[OWN:, :].astype(F32)
    step = (inc_next[...].astype(F32) - increment).astype(BF16)
    step_bar = dot_t(step, w[OUTPUT])

    all_v.wait_recv()
    act[...] = (slope[...] * (loc_v[...] + dot(far[...], halo_v[...]))).astype(BF16)
    tangent_sum = dot(near_t[OWN:, :], act[...]).astype(BF16)
    node_tangent = (node_slope * (node[OWN:] + dot(tangent_sum, w_mi))).astype(BF16)
    node_bar = node_slope * (step_bar - dot(node_tangent, w_oo))
    node_bar = jnp.where(last, 0.0, node_bar).astype(BF16)
    edge_in = dot(node_bar, turned[0]).astype(BF16)
    act[...] = (slope[...] * dot(near[:, OWN:], edge_in)).astype(BF16)
    half = HALO // 2
    for at in (half, 0):
        ret_out[at : at + half, :] = dot(far_t[at : at + half, :], act[...]).astype(BF16)
        for b in range(at // SLOT, min((at + half) // SLOT, len(AWAY))):
            send(block(ret_out, b), part(ret_in, me), 2, {"mesh": sources[b]})

    tangent = (increment + dot(node_tangent, w[OUTPUT])).astype(BF16)
    tan_out[...] = tangent

    @pl.when(jnp.logical_not(last))
    def _():
        send(tan_out, before, 4, after)

    sums = dot(near_t[...], act[...])
    cotangent = (inc_next[...].astype(F32) - tangent.astype(F32)).astype(BF16).astype(F32)
    adjoint = jnp.where(last, 0.0, cotangent)
    adjoint = adjoint + dot_t(node_bar, w[NODE]) + dot_t(sums[OWN:].astype(BF16), w[RECEIVE])

    pl.when(jnp.logical_not(first))(all_tan.wait_recv)
    forward = (increment - before[...].astype(F32)).astype(BF16)
    fi_ref[0] = forward
    rest = forward.astype(F32) - adjoint

    all_back.wait_recv()
    owned = (sums[:OWN] + dot(pick_t[...], ret_in[...])).astype(BF16)
    ni_ref[0] = (rest - dot(owned, turned[1])).astype(BF16)

    all_x.wait_send()
    all_v.wait_send()
    all_back.wait_send()
    pl.when(jnp.logical_not(first))(all_inc.wait_send)
    pl.when(jnp.logical_not(last))(all_tan.wait_send)


def store(fi_vmem, ni_vmem, fi_hbm, ni_hbm, sem):
    copies = [
        pltpu.make_async_copy(fi_vmem, fi_hbm, sem.at[0]),
        pltpu.make_async_copy(ni_vmem, ni_hbm, sem.at[1]),
    ]
    for copy in copies:
        copy.start()
    for copy in copies:
        copy.wait()


def on_device(
    trajectory,
    increments,
    weight_send,
    weight_receive,
    weight_message,
    weight_node,
    weight_inbox,
    weight_output,
    senders,
    receivers,
    send_table,
):
    image = jax.ShapeDtypeStruct((1, OWN, WIDTH), BF16)
    rows = lambda n: pltpu.VMEM((n, WIDTH), BF16)
    operands = (
        trajectory,
        increments,
        weight_send,
        weight_receive,
        weight_message,
        weight_node,
        weight_inbox,
        weight_output,
        senders.reshape(EDGES // LANES, LANES),
        receivers.reshape(EDGES // LANES, LANES),
        send_table.reshape(HALO // LANES, LANES),
    )
    images = pl.pallas_call(
        kernel,
        out_shape=(pltpu.VMEM(image.shape, BF16),) * 2,
        in_specs=[pl.BlockSpec(memory_space=pl.ANY)] * 11,
        out_specs=(pl.BlockSpec(memory_space=pltpu.VMEM),) * 2,
        scratch_shapes=[
            rows(2 * OWN),
            pltpu.VMEM((6, WIDTH, WIDTH), BF16),
            pltpu.VMEM((2, EDGES // LANES, LANES), jnp.int32),
            pltpu.VMEM((HALO // LANES, LANES), jnp.int32),
            pltpu.VMEM((HALO, OWN), BF16),
            pltpu.VMEM((OWN, HALO), BF16),
            pltpu.VMEM((EDGES, 2 * OWN), BF16),
            pltpu.VMEM((EDGES, HALO), BF16),
            pltpu.VMEM((2 * OWN, EDGES), BF16),
            pltpu.VMEM((HALO, EDGES), BF16),
            rows(HALO),
            rows(HALO),
            rows(HALO),
            rows(HALO),
            rows(OWN),
            rows(OWN),
            rows(OWN),
            rows(HALO),
            rows(HALO),
            pltpu.VMEM((EDGES, WIDTH), F32),
            pltpu.VMEM((EDGES, WIDTH), F32),
            pltpu.VMEM((EDGES, WIDTH), F32),
            pltpu.VMEM((EDGES, WIDTH), BF16),
            pltpu.VMEM((2, WIDTH, WIDTH), BF16),
            pltpu.SemaphoreType.DMA((6,)),
            pltpu.SemaphoreType.DMA((5,)),
            pltpu.SemaphoreType.DMA((5,)),
        ],
        compiler_params=pltpu.CompilerParams(
            collective_id=0, has_side_effects=True, vmem_limit_bytes=40 << 20
        ),
    )(*[pltpu.with_memory_space_constraint(operand, pltpu.HBM) for operand in operands])
    return pl.pallas_call(
        store,
        out_shape=(image, image),
        in_specs=[pl.BlockSpec(memory_space=pltpu.VMEM)] * 2,
        out_specs=(pl.BlockSpec(memory_space=pl.ANY),) * 2,
        scratch_shapes=[pltpu.SemaphoreType.DMA((2,))],
        compiler_params=pltpu.CompilerParams(vmem_limit_bytes=4 << 20),
    )(*images)


def solution(mesh):
    nodes = P("tm", "mesh", None)
    in_specs = (nodes, nodes) + (P(),) * 6 + (P("mesh"),) * 3
    return jax.shard_map(
        on_device, mesh=mesh, in_specs=in_specs, out_specs=(nodes, nodes), check_vma=False
    )
```
